32 devices in a mesh: groups: 2 (over y), frame: 4 (over z), head: 2 (over x), pair: 2 (over core).
Axes of the slice: x: 2, y: 2, z: 4, core: 2. Of those that a mesh axis runs over, the one named last changes fastest.
Arguments:
- queries: bfloat16 [16, 1024, 3072], P(('groups', 'frame'), None, ('head', 'pair')), parts along dimension 0, may hold values from -6 to 6
- key_states: bfloat16 [16, 1024, 3072], P(('groups', 'frame'), None, ('head', 'pair')), parts along dimension 0, may hold values from -6 to 6
- value_states: bfloat16 [16, 1024, 3072], P(('groups', 'frame'), None, ('head', 'pair')), parts along dimension 0, may hold values from -6 to 6
- old_feature: bfloat16 [16, 1024, 3072], P(('groups', 'frame'), None, ('head', 'pair')), parts along dimension 0, may hold values from -4 to 4
- head_class: int32 [48], replicated, may hold values 0 or 1
- block_index: int32 [48, 64, 4], replicated, may hold values from 0 to 7, as said below
Outputs:
- feature: bfloat16 [16, 1024, 3072], P(('groups', 'frame'), None, ('head', 'pair')), parts along dimension 0
- derivative: bfloat16 [16, 1024, 3072], P(('groups', 'frame'), None, ('head', 'pair')), parts along dimension 0
The draws below stay inside these ranges and needn't reach their ends.
There are 2 independent parts, one for each index of `groups`. The reference program is written for one: setup_inputs(seed, part) draws one part's arguments, and reference() takes and returns one part's arrays. A program takes and returns all parts, laid end to end along the dimension named above; an argument that names none is the same for every part. Nothing has to cross between parts.
Inputs may be any that keep to these rules, and one draw needn't show every extreme that they name: `block_index`: each list names 4 different offsets within the query block's group; the first is the query block's own offset.
All inputs are finite; a program needn't handle non-finite values.
Results may differ from the reference program's by a relative error of at most 0.0047.
Values may be sent and summed in bfloat16 or wider, within the bound.
A program may use at most 128 MiB of HBM per device.

```python
import jax
import jax.numpy as jnp
from jax import lax

HEADS = 48
HEAD_DIM = 64
POS = 1024
BLOCK = 128
GROUP = 8
LISTED = 4
INTERVAL = 5
FRAMES = 8
NB = 64
WIDTH = 3072


def draw_queries(key, part):
    key = jax.random.fold_in(key, 11)
    return jnp.clip(jax.random.normal(key, (FRAMES, POS, HEADS * HEAD_DIM)), -6.0, 6.0).astype(jnp.bfloat16)


def draw_key_states(key, part):
    key = jax.random.fold_in(key, 12)
    return jnp.clip(jax.random.normal(key, (FRAMES, POS, HEADS * HEAD_DIM)), -6.0, 6.0).astype(jnp.bfloat16)


def draw_block_index(key, part):
    key = jax.random.fold_in(key, 21)
    own_offset = jnp.arange(NB, dtype=jnp.int32) % GROUP
    scores = jax.random.randint(key, (HEADS, NB, GROUP - 1), 0, 1 << 20) * GROUP + jnp.arange(GROUP - 1, dtype=jnp.int32)
    picked = jnp.argsort(scores, axis=-1)[:, :, :LISTED - 1].astype(jnp.int32)
    others = picked + (picked >= own_offset[None, :, None]).astype(jnp.int32)
    leading = jnp.broadcast_to(own_offset[None, :, None], (HEADS, NB, 1))
    return jnp.concatenate([leading, others], axis=-1).astype(jnp.int32)


def touch_ends(entries, key, low, largest):
    place = [jax.random.randint(jax.random.fold_in(key, axis), (), 0, length) for axis, length in enumerate(entries.shape)]
    main_axis = entries.shape.index(max(entries.shape))
    beside = place[:main_axis] + [(place[main_axis] + 1) % entries.shape[main_axis]] + place[main_axis + 1:]
    return entries.at[tuple(place)].set(low).at[tuple(beside)].set(largest)


def block_scale(stream_key, extent, shards, low, high):
    def one(axis_at, parts):
        heights = jax.random.uniform(jax.random.fold_in(jax.random.fold_in(stream_key, 6), axis_at), (parts,), jnp.float32, low / len(shards), high / len(shards))
        return jnp.repeat(jnp.exp(heights), extent[axis_at] // parts).reshape((-1,) + (1,) * (len(extent) - axis_at - 1))

    loudness = one(*shards[0])
    for cut in shards[1:]:
        loudness = loudness * one(*cut)
    return loudness


def noise(own_key, extent, width, most, cuts=(), held_as=jnp.bfloat16):
    result = jax.random.normal(own_key, extent, jnp.float32) * width
    if len(cuts) > 0:
        result = block_scale(own_key, extent, cuts, -0.22, 0.18) * result
    return jnp.clip(result, min=-most, max=most).astype(held_as)


def setup_inputs(seed: int = 0, part: int = 0) -> dict:
    arg_keys = jax.random.split(jax.random.key(seed), 7)
    part_splits = jax.random.split(jax.random.fold_in(arg_keys[6], part), 7)
    return {
        "queries": draw_queries(jax.random.fold_in(jax.random.fold_in(arg_keys[6], part), 71), part),
        "key_states": draw_key_states(jax.random.fold_in(jax.random.fold_in(arg_keys[6], part), 71), part),
        "value_states": noise(part_splits[2], (FRAMES, POS, WIDTH), 1.0, 6.0, ((0, 4), (2, 4))),
        "old_feature": noise(part_splits[3], (FRAMES, POS, WIDTH), 0.5, 4.0, ((0, 4), (2, 4))),
        "head_class": touch_ends((jax.random.randint(arg_keys[4], (HEADS,), 0, 3) < 1).astype(jnp.int32), jax.random.fold_in(arg_keys[4], 1), 0, 1),
        "block_index": draw_block_index(jax.random.fold_in(arg_keys[6], 71), part),
    }


def softmax_read(scores, value_tile, keep_mask):
    if keep_mask is not None:
        scores = jnp.where(keep_mask, scores, -jnp.inf)
    row_max = jnp.max(scores, axis=-1, keepdims=True)
    exponent = jnp.exp(scores - row_max)
    weights = lax.optimization_barrier(exponent.astype(jnp.bfloat16))
    row_sum = jnp.sum(exponent, axis=-1, keepdims=True)
    blended = jnp.einsum("...qk,...kd->...qd", weights.astype(jnp.float32), value_tile.astype(jnp.float32))
    return blended / row_sum


def spatial_head(query_tile, key_tile, value_tile, block_lists):
    scores = jnp.einsum("fpd,fqd->fpq", query_tile.astype(jnp.float32), key_tile.astype(jnp.float32)) * HEAD_DIM ** -0.5
    return softmax_read(scores, value_tile, None)


def position_major(tensor):
    return jnp.swapaxes(tensor, 0, 1).reshape(-1, GROUP * BLOCK, HEAD_DIM)


def temporal_head(query_tile, key_tile, value_tile, block_lists):
    query_groups = position_major(query_tile)
    key_groups = position_major(key_tile)
    value_groups = position_major(value_tile)
    group_count = query_groups.shape[0]
    scores = jnp.einsum("gqd,gkd->gqk", query_groups.astype(jnp.float32), key_groups.astype(jnp.float32)) * HEAD_DIM ** -0.5
    offsets = jnp.arange(GROUP, dtype=jnp.int32)
    listed = block_lists.reshape(group_count, GROUP, LISTED)
    allowed = jnp.any(listed[:, :, :, None] == offsets[None, None, None, :], axis=2)
    keep_mask = jnp.broadcast_to(allowed[:, :, None, :, None], (group_count, GROUP, BLOCK, GROUP, BLOCK))
    keep_mask = keep_mask.reshape(group_count, GROUP * BLOCK, GROUP * BLOCK)
    blended = softmax_read(scores, value_groups, keep_mask)
    return jnp.swapaxes(blended.reshape(POS, FRAMES, HEAD_DIM), 0, 1)


def reference(queries, key_states, value_states, old_feature, head_class, block_index):
    def per_head(tensor):
        return jnp.moveaxis(tensor.reshape(FRAMES, POS, HEADS, HEAD_DIM), 2, 0)

    def attend_head(pieces):
        query_tile, key_tile, value_tile, flag, block_lists = pieces
        return lax.cond(flag == 1, temporal_head, spatial_head, query_tile, key_tile, value_tile, block_lists)

    outputs = lax.map(attend_head, (per_head(queries), per_head(key_states), per_head(value_states), head_class, block_index))
    blended = jnp.moveaxis(outputs, 0, 2).reshape(FRAMES, POS, HEADS * HEAD_DIM)
    feature = blended.astype(jnp.bfloat16)
    kept = lax.optimization_barrier(feature).astype(jnp.float32)
    derivative = ((kept - old_feature.astype(jnp.float32)) / INTERVAL).astype(jnp.bfloat16)
    return feature, derivative
```

```python
import functools

import jax
import jax.numpy as jnp
from jax import lax
from jax.experimental import pallas as pl
from jax.experimental.pallas import tpu as pltpu
from jax.sharding import PartitionSpec as P

HEAD_DIM = 64
BLOCK = 128
GROUP = 8
LISTED = 4
INTERVAL = 5


def softmax_read(query_tile, key_tile, value_tile, keep_mask):
    scores = jnp.einsum(
        "...qd,...kd->...qk", query_tile, key_tile, preferred_element_type=jnp.float32
    ) * HEAD_DIM ** (-0.5)
    if keep_mask is not None:
        scores = jnp.where(keep_mask, scores, -jnp.inf)
    row_max = jnp.max(scores, axis=-1, keepdims=True)
    exponent = jnp.exp(scores - row_max)
    row_sum = jnp.sum(exponent, axis=-1, keepdims=True)
    weights = exponent.astype(jnp.bfloat16)
    blended = jnp.einsum(
        "...qk,...kd->...qd", weights, value_tile, preferred_element_type=jnp.float32
    )
    return blended / row_sum


def spatial_part(queries, key_states, value_states, head_count):
    frames_dev, positions, row_width = queries.shape

    def as_items(tensor):
        shaped = tensor.reshape(frames_dev, positions, head_count, HEAD_DIM)
        return shaped.transpose(0, 2, 1, 3).reshape(frames_dev * head_count, positions, HEAD_DIM)

    def spatial_attend_one(pieces):
        return softmax_read(pieces[0], pieces[1], pieces[2], None)

    blended = lax.map(
        spatial_attend_one, (as_items(queries), as_items(key_states), as_items(value_states))
    )
    blended = blended.reshape(frames_dev, head_count, positions, HEAD_DIM).transpose(0, 2, 1, 3)
    return blended.reshape(frames_dev, positions, row_width)


def temporal_part(queries, key_states, value_states, block_lists, head_count):
    frames, local_span, row_width = queries.shape
    group_span = GROUP * BLOCK // frames
    group_count = local_span // group_span

    def as_items(tensor):
        shaped = tensor.reshape(frames, group_count, group_span, head_count, HEAD_DIM)
        return shaped.transpose(1, 3, 0, 2, 4).reshape(
            group_count * head_count, frames * group_span, HEAD_DIM
        )

    listed_all = block_lists.reshape(head_count, group_count, GROUP, LISTED).transpose(1, 0, 2, 3)
    listed_all = listed_all.reshape(group_count * head_count, GROUP, LISTED)
    offsets = jnp.arange(GROUP, dtype=jnp.int32)
    block_of = (
        jnp.arange(group_span, dtype=jnp.int32)[None, :] * frames
        + jnp.arange(frames, dtype=jnp.int32)[:, None]
    ).reshape(-1) // BLOCK
    member = (block_of[:, None] == offsets[None, :]).astype(jnp.float32)

    def temporal_attend_one(pieces):
        query_tile, key_tile, value_tile, listed = pieces
        allowed = jnp.any(listed[:, :, None] == offsets[None, None, :], axis=1).astype(jnp.float32)
        keep_mask = jnp.dot(jnp.dot(member, allowed), member.T) > 0.5
        return softmax_read(query_tile, key_tile, value_tile, keep_mask)

    blended = lax.map(
        temporal_attend_one,
        (as_items(queries), as_items(key_states), as_items(value_states), listed_all),
    )
    blended = blended.reshape(group_count, head_count, frames, group_span, HEAD_DIM).transpose(
        2, 0, 3, 1, 4
    )
    return blended.reshape(frames, local_span, row_width).astype(jnp.bfloat16)


def per_device_plain(queries, key_states, value_states, old_feature, head_class, block_index):
    frames_dev, positions, row_width = queries.shape
    head_count = row_width // HEAD_DIM
    pair_count = lax.axis_size("pair")
    sources = lax.axis_size("frame")
    frames = frames_dev * sources
    group_span = GROUP * BLOCK // frames
    head_start = (lax.axis_index("head") * pair_count + lax.axis_index("pair")) * head_count
    spatial = spatial_part(queries, key_states, value_states, head_count)
    local_span = positions // sources
    arrived = (
        lax.all_to_all(queries, "frame", split_axis=1, concat_axis=0, tiled=True),
        lax.all_to_all(key_states, "frame", split_axis=1, concat_axis=0, tiled=True),
        lax.all_to_all(value_states, "frame", split_axis=1, concat_axis=0, tiled=True),
    )
    first_position = lax.axis_index("frame") * local_span
    block_lists = lax.dynamic_slice(
        block_index,
        (head_start, first_position // group_span * GROUP, 0),
        (head_count, local_span // group_span * GROUP, LISTED),
    )
    temporal = temporal_part(arrived[0], arrived[1], arrived[2], block_lists, head_count)
    returned = lax.all_to_all(temporal, "frame", split_axis=0, concat_axis=1, tiled=True)
    column_class = jnp.repeat(
        lax.dynamic_slice_in_dim(head_class, head_start, head_count), HEAD_DIM
    )
    feature = jnp.where(column_class[None, None, :] == 1, returned, spatial.astype(jnp.bfloat16))
    kept = lax.optimization_barrier(feature).astype(jnp.float32)
    derivative = ((kept - old_feature.astype(jnp.float32)) / INTERVAL).astype(jnp.bfloat16)
    return (feature, derivative)


PAIR = 2 * HEAD_DIM
LOG2E = 1.4426950408889634
NT_DIMS = (((1,), (1,)), ((), ()))


def params():
    return pltpu.CompilerParams(vmem_limit_bytes=40 * 1024 * 1024)


def lane_half(rows):
    return lax.broadcasted_iota(jnp.int32, (rows, PAIR), 1) >= HEAD_DIM


def one_head(query_pair, upper, half, key_tile, value_ones):
    own = upper if half else jnp.logical_not(upper)
    scaled = jnp.where(own, query_pair * HEAD_DIM ** (-0.5), 0.0).astype(jnp.bfloat16)
    scores = lax.dot_general(scaled, key_tile, NT_DIMS, preferred_element_type=jnp.float32)
    row_max = jnp.max(scores, axis=-1, keepdims=True)
    weights = jnp.exp2((scores - row_max) * LOG2E).astype(jnp.bfloat16)
    return jnp.dot(weights, value_ones, preferred_element_type=jnp.float32)


def divide_pair(upper, low, high):
    blended = jnp.where(upper, high, low)
    sums = pltpu.roll(jnp.where(upper, low, high), HEAD_DIM, 1)
    return blended / sums


def with_ones(value_pair, half):
    upper = lane_half(value_pair.shape[0])
    own = upper if half else jnp.logical_not(upper)
    return jnp.where(own, value_pair.astype(jnp.float32), 1.0).astype(jnp.bfloat16)


def spatial_kernel(tile, class_ref, q_ref, k_ref, v_ref, out_ref, acc_ref):
    pair = pl.program_id(1)
    positions = q_ref.shape[1]
    upper = lane_half(tile)
    for half in range(2):

        @pl.when(class_ref[2 * pair + half] == 0)
        def _():
            value_ones = with_ones(v_ref[0], half)
            for at in range(0, positions, tile):
                acc_ref[half, pl.ds(at, tile), :] = one_head(
                    q_ref[0, pl.ds(at, tile), :].astype(jnp.float32),
                    upper, half, k_ref[0], value_ones,
                )

    for at in range(0, positions, tile):
        out_ref[0, pl.ds(at, tile), :] = divide_pair(
            upper, acc_ref[0, pl.ds(at, tile), :], acc_ref[1, pl.ds(at, tile), :]
        ).astype(jnp.bfloat16)


def spatial_call(classes, queries, key_states, value_states):
    frames_dev, positions, row_width = queries.shape
    pairs = row_width // PAIR
    spec = pl.BlockSpec((1, positions, PAIR), lambda f, p, c: (f, 0, p))
    return pl.pallas_call(
        functools.partial(spatial_kernel, 256),
        grid_spec=pltpu.PrefetchScalarGridSpec(
            num_scalar_prefetch=1,
            grid=(frames_dev, pairs),
            in_specs=[spec] * 3,
            out_specs=spec,
            scratch_shapes=[pltpu.VMEM((2, positions, PAIR), jnp.float32)],
        ),
        out_shape=jax.ShapeDtypeStruct(queries.shape, jnp.bfloat16),
        compiler_params=params(),
        cost_estimate=pl.CostEstimate(
            flops=frames_dev * 2 * pairs * positions * positions * HEAD_DIM * 16,
            bytes_accessed=8 * frames_dev * positions * row_width,
            transcendentals=frames_dev * 2 * pairs * positions * positions,
        ),
        name="spatial",
    )(classes, queries, key_states, value_states)


def moved(block, parity):
    wide = block.astype(jnp.float32)
    return jnp.where(parity == 1, pltpu.roll(wide, HEAD_DIM, 1), wide)


def pack_kernel(heads_ref, qa, ka, va, qb, kb, vb, out_ref):
    slot = 2 * pl.program_id(0)
    left_parity = lax.rem(heads_ref[slot], 2)
    right_parity = 1 - lax.rem(heads_ref[slot + 1], 2)
    positions = qa.shape[1]
    upper = lane_half(positions)
    for at, (left, right) in enumerate(((qa, qb), (ka, kb), (va, vb))):
        both = jnp.where(upper, moved(right[0], right_parity), moved(left[0], left_parity))
        out_ref[:, at, 0, 0] = both.astype(jnp.bfloat16).reshape(
            out_ref.shape[0], positions // out_ref.shape[0], PAIR
        )


def pack_call(slot_pairs, sources, heads, tensors):
    frames_dev, positions, _ = tensors[0].shape
    span = positions // sources
    left = pl.BlockSpec((1, positions, PAIR), lambda t, f, h: (f, 0, h[2 * t] // 2))
    right = pl.BlockSpec((1, positions, PAIR), lambda t, f, h: (f, 0, h[2 * t + 1] // 2))
    return pl.pallas_call(
        pack_kernel,
        grid_spec=pltpu.PrefetchScalarGridSpec(
            num_scalar_prefetch=1,
            grid=(slot_pairs, frames_dev),
            in_specs=[left] * 3 + [right] * 3,
            out_specs=pl.BlockSpec(
                (sources, 3, 1, 1, span, PAIR), lambda t, f, h: (0, 0, t, f, 0, 0)
            ),
        ),
        out_shape=jax.ShapeDtypeStruct(
            (sources, 3, slot_pairs, frames_dev, span, PAIR), jnp.bfloat16
        ),
        compiler_params=params(),
        name="pack",
    )(heads, *tensors, *tensors)


def temporal_kernel(list_ref, q_ref, k_ref, v_ref, out_ref, key_ref, value_ref):
    pair = pl.program_id(0)
    groups = pl.num_programs(1)
    group = pl.program_id(1)
    step = q_ref.shape[4] // GROUP
    shape = (q_ref.shape[0], q_ref.shape[3], step, PAIR)
    upper = lane_half(BLOCK)
    for block in range(GROUP):
        rows = pl.ds(block * BLOCK, BLOCK)
        here = pl.ds(block * step, step)
        key_ref[rows, :] = k_ref[:, 0, 0, :, here, :].reshape(BLOCK, PAIR)
        value_tile = v_ref[:, 0, 0, :, here, :].reshape(BLOCK, PAIR)
        for half in range(2):
            value_ref[half, rows, :] = with_ones(value_tile, half)
    for block in range(GROUP):
        here = pl.ds(block * step, step)
        query_tile = q_ref[:, 0, 0, :, here, :].reshape(BLOCK, PAIR).astype(jnp.float32)
        parts = []
        for half in range(2):
            base = (((2 * pair + half) * groups + group) * GROUP + block) * LISTED
            rows = [
                pl.ds(pl.multiple_of(list_ref[base + at] * BLOCK, BLOCK), BLOCK)
                for at in range(LISTED)
            ]
            key_tile = jnp.concatenate([key_ref[row, :] for row in rows], axis=0)
            value_ones = jnp.concatenate([value_ref[half, row, :] for row in rows], axis=0)
            parts.append(one_head(query_tile, upper, half, key_tile, value_ones))
        out_ref[:, 0, :, here, :] = (
            divide_pair(upper, parts[0], parts[1]).astype(jnp.bfloat16).reshape(shape)
        )


def temporal_call(lists, arrived):
    sources, _, slot_pairs, frames_dev, span, _ = arrived.shape
    group_span = GROUP * BLOCK // (sources * frames_dev)
    groups = span // group_span
    size = (sources, 1, 1, frames_dev, group_span, PAIR)

    def spec(tensor):
        return pl.BlockSpec(size, lambda t, g, l: (0, tensor, t, 0, g, 0))

    return pl.pallas_call(
        temporal_kernel,
        grid_spec=pltpu.PrefetchScalarGridSpec(
            num_scalar_prefetch=1,
            grid=(slot_pairs, groups),
            in_specs=[spec(0), spec(1), spec(2)],
            out_specs=pl.BlockSpec(
                (sources, 1, frames_dev, group_span, PAIR), lambda t, g, l: (0, t, 0, g, 0)
            ),
            scratch_shapes=[
                pltpu.VMEM((GROUP * BLOCK, PAIR), jnp.bfloat16),
                pltpu.VMEM((2, GROUP * BLOCK, PAIR), jnp.bfloat16),
            ],
        ),
        out_shape=jax.ShapeDtypeStruct(
            (sources, slot_pairs, frames_dev, span, PAIR), jnp.bfloat16
        ),
        compiler_params=params(),
        name="temporal",
    )(lists, arrived, arrived, arrived)


def merge_kernel(class_ref, slot_ref, spatial_ref, old_ref, a_ref, b_ref, feature_ref, derivative_ref):
    pair = pl.program_id(1)
    positions = old_ref.shape[1]
    upper = lane_half(positions)
    low_parity = lax.rem(slot_ref[2 * pair], 2)
    high_parity = 1 - lax.rem(slot_ref[2 * pair + 1], 2)
    low = moved(a_ref[:, 0, 0].reshape(positions, PAIR), low_parity)
    high = moved(b_ref[:, 0, 0].reshape(positions, PAIR), high_parity)
    chosen = jnp.where(upper, class_ref[2 * pair + 1], class_ref[2 * pair]) == 1
    kept = jnp.where(chosen, jnp.where(upper, high, low), spatial_ref[0].astype(jnp.float32))
    feature_ref[0] = kept.astype(jnp.bfloat16)
    derivative_ref[0] = ((kept - old_ref[0].astype(jnp.float32)) / INTERVAL).astype(jnp.bfloat16)


def merge_call(classes, slots, spatial, old_feature, returned):
    frames_dev, positions, row_width = spatial.shape
    sources, _, _, span, _ = returned.shape
    spec = pl.BlockSpec((1, positions, PAIR), lambda f, p, c, s: (f, 0, p))
    size = (sources, 1, 1, span, PAIR)
    low = pl.BlockSpec(size, lambda f, p, c, s: (0, s[2 * p] // 2, f, 0, 0))
    high = pl.BlockSpec(size, lambda f, p, c, s: (0, s[2 * p + 1] // 2, f, 0, 0))
    shape = jax.ShapeDtypeStruct(spatial.shape, jnp.bfloat16)
    return pl.pallas_call(
        merge_kernel,
        grid_spec=pltpu.PrefetchScalarGridSpec(
            num_scalar_prefetch=2,
            grid=(frames_dev, row_width // PAIR),
            in_specs=[spec, spec, low, high],
            out_specs=[spec, spec],
        ),
        out_shape=(shape, shape),
        compiler_params=params(),
        name="merge",
    )(classes, slots, spatial, old_feature, returned, returned)


def per_device(queries, key_states, value_states, old_feature, head_class, block_index):
    frames_dev, positions, row_width = queries.shape
    head_count = row_width // HEAD_DIM
    pair_count = lax.axis_size("pair")
    sources = lax.axis_size("frame")
    frames = frames_dev * sources
    span = positions // sources
    group_span = GROUP * BLOCK // frames
    if row_width % PAIR or BLOCK % (frames * 16) or span % group_span:
        return per_device_plain(
            queries, key_states, value_states, old_feature, head_class, block_index
        )
    holder = lax.axis_index("head") * pair_count + lax.axis_index("pair")
    head_start = holder * head_count
    classes = lax.dynamic_slice_in_dim(head_class, head_start, head_count)
    is_temporal = (classes == 1).astype(jnp.int32)
    slots = jnp.where(is_temporal == 1, jnp.cumsum(is_temporal) - 1, 0)
    heads = jnp.sum(
        jnp.where(
            (slots[None, :] == jnp.arange(head_count)[:, None]) & (is_temporal[None, :] == 1),
            jnp.arange(head_count, dtype=jnp.int32)[None, :],
            0,
        ),
        axis=1,
    ).astype(jnp.int32)
    most = jnp.max(jnp.sum((head_class == 1).reshape(-1, head_count).astype(jnp.int32), axis=1))
    groups = span // group_span
    lists = lax.dynamic_slice(
        block_index,
        (head_start, lax.axis_index("frame") * groups * GROUP, 0),
        (head_count, groups * GROUP, LISTED),
    ).reshape(head_count, -1)
    lists = jnp.take(lists, heads, axis=0).reshape(-1)
    pick = is_temporal

    def none_temporal(queries, key_states, value_states, old_feature, pick, slots, heads, lists):
        feature = spatial_call(pick, queries, key_states, value_states)
        kept = feature.astype(jnp.float32)
        derivative = ((kept - old_feature.astype(jnp.float32)) / INTERVAL).astype(jnp.bfloat16)
        return feature, derivative

    def some_temporal(slot_pairs):
        def run(queries, key_states, value_states, old_feature, pick, slots, heads, lists):
            packed = pack_call(slot_pairs, sources, heads, (queries, key_states, value_states))
            arrived = lax.all_to_all(packed, "frame", split_axis=0, concat_axis=0, tiled=True)
            spatial = spatial_call(pick, queries, key_states, value_states)
            temporal = temporal_call(lists, arrived)
            returned = lax.all_to_all(temporal, "frame", split_axis=0, concat_axis=0, tiled=True)
            return merge_call(pick, slots, spatial, old_feature, returned)

        return run

    branches = [none_temporal] + [some_temporal(n + 1) for n in range((head_count + 1) // 2)]
    return lax.switch(
        (most + 1) // 2, branches,
        queries, key_states, value_states, old_feature, pick, slots, heads, lists,
    )


def solution(mesh):
    in_specs = (
        P(("groups", "frame"), None, ("head", "pair")),
        P(("groups", "frame"), None, ("head", "pair")),
        P(("groups", "frame"), None, ("head", "pair")),
        P(("groups", "frame"), None, ("head", "pair")),
        P(),
        P(),
    )
    out_specs = (
        P(("groups", "frame"), None, ("head", "pair")),
        P(("groups", "frame"), None, ("head", "pair")),
    )
    return jax.shard_map(
        per_device, mesh=mesh, in_specs=in_specs, out_specs=out_specs, check_vma=False
    )
```

```python
import functools

import jax
import jax.numpy as jnp
from jax import lax
from jax.experimental import pallas as pl
from jax.experimental.pallas import tpu as pltpu
from jax.sharding import PartitionSpec as P

HEAD_DIM = 64
BLOCK = 128
GROUP = 8
LISTED = 4
INTERVAL = 5


def softmax_read(query_tile, key_tile, value_tile, keep_mask):
    scores = jnp.einsum(
        "...qd,...kd->...qk", query_tile, key_tile, preferred_element_type=jnp.float32
    ) * HEAD_DIM ** (-0.5)
    if keep_mask is not None:
        scores = jnp.where(keep_mask, scores, -jnp.inf)
    row_max = jnp.max(scores, axis=-1, keepdims=True)
    exponent = jnp.exp(scores - row_max)
    row_sum = jnp.sum(exponent, axis=-1, keepdims=True)
    weights = exponent.astype(jnp.bfloat16)
    blended = jnp.einsum(
        "...qk,...kd->...qd", weights, value_tile, preferred_element_type=jnp.float32
    )
    return blended / row_sum


def spatial_part(queries, key_states, value_states, head_count):
    frames_dev, positions, row_width = queries.shape

    def as_items(tensor):
        shaped = tensor.reshape(frames_dev, positions, head_count, HEAD_DIM)
        return shaped.transpose(0, 2, 1, 3).reshape(frames_dev * head_count, positions, HEAD_DIM)

    def spatial_attend_one(pieces):
        return softmax_read(pieces[0], pieces[1], pieces[2], None)

    blended = lax.map(
        spatial_attend_one, (as_items(queries), as_items(key_states), as_items(value_states))
    )
    blended = blended.reshape(frames_dev, head_count, positions, HEAD_DIM).transpose(0, 2, 1, 3)
    return blended.reshape(frames_dev, positions, row_width)


def temporal_part(queries, key_states, value_states, block_lists, head_count):
    frames, local_span, row_width = queries.shape
    group_span = GROUP * BLOCK // frames
    group_count = local_span // group_span

    def as_items(tensor):
        shaped = tensor.reshape(frames, group_count, group_span, head_count, HEAD_DIM)
        return shaped.transpose(1, 3, 0, 2, 4).reshape(
            group_count * head_count, frames * group_span, HEAD_DIM
        )

    listed_all = block_lists.reshape(head_count, group_count, GROUP, LISTED).transpose(1, 0, 2, 3)
    listed_all = listed_all.reshape(group_count * head_count, GROUP, LISTED)
    offsets = jnp.arange(GROUP, dtype=jnp.int32)
    block_of = (
        jnp.arange(group_span, dtype=jnp.int32)[None, :] * frames
        + jnp.arange(frames, dtype=jnp.int32)[:, None]
    ).reshape(-1) // BLOCK
    member = (block_of[:, None] == offsets[None, :]).astype(jnp.float32)

    def temporal_attend_one(pieces):
        query_tile, key_tile, value_tile, listed = pieces
        allowed = jnp.any(listed[:, :, None] == offsets[None, None, :], axis=1).astype(jnp.float32)
        keep_mask = jnp.dot(jnp.dot(member, allowed), member.T) > 0.5
        return softmax_read(query_tile, key_tile, value_tile, keep_mask)

    blended = lax.map(
        temporal_attend_one,
        (as_items(queries), as_items(key_states), as_items(value_states), listed_all),
    )
    blended = blended.reshape(group_count, head_count, frames, group_span, HEAD_DIM).transpose(
        2, 0, 3, 1, 4
    )
    return blended.reshape(frames, local_span, row_width).astype(jnp.bfloat16)


def per_device_plain(queries, key_states, value_states, old_feature, head_class, block_index):
    frames_dev, positions, row_width = queries.shape
    head_count = row_width // HEAD_DIM
    pair_count = lax.axis_size("pair")
    sources = lax.axis_size("frame")
    frames = frames_dev * sources
    group_span = GROUP * BLOCK // frames
    head_start = (lax.axis_index("head") * pair_count + lax.axis_index("pair")) * head_count
    spatial = spatial_part(queries, key_states, value_states, head_count)
    local_span = positions // sources
    arrived = (
        lax.all_to_all(queries, "frame", split_axis=1, concat_axis=0, tiled=True),
        lax.all_to_all(key_states, "frame", split_axis=1, concat_axis=0, tiled=True),
        lax.all_to_all(value_states, "frame", split_axis=1, concat_axis=0, tiled=True),
    )
    first_position = lax.axis_index("frame") * local_span
    block_lists = lax.dynamic_slice(
        block_index,
        (head_start, first_position // group_span * GROUP, 0),
        (head_count, local_span // group_span * GROUP, LISTED),
    )
    temporal = temporal_part(arrived[0], arrived[1], arrived[2], block_lists, head_count)
    returned = lax.all_to_all(temporal, "frame", split_axis=0, concat_axis=1, tiled=True)
    column_class = jnp.repeat(
        lax.dynamic_slice_in_dim(head_class, head_start, head_count), HEAD_DIM
    )
    feature = jnp.where(column_class[None, None, :] == 1, returned, spatial.astype(jnp.bfloat16))
    kept = lax.optimization_barrier(feature).astype(jnp.float32)
    derivative = ((kept - old_feature.astype(jnp.float32)) / INTERVAL).astype(jnp.bfloat16)
    return (feature, derivative)


PAIR = 2 * HEAD_DIM
LOG2E = 1.4426950408889634
NT_DIMS = (((1,), (1,)), ((), ()))


def params():
    return pltpu.CompilerParams(vmem_limit_bytes=40 * 1024 * 1024)


def lane_half(rows):
    return lax.broadcasted_iota(jnp.int32, (rows, PAIR), 1) >= HEAD_DIM


def one_head(query_pair, upper, half, key_tile, value_ones):
    own = upper if half else jnp.logical_not(upper)
    scaled = jnp.where(own, query_pair * HEAD_DIM ** (-0.5), 0.0).astype(jnp.bfloat16)
    scores = lax.dot_general(scaled, key_tile, NT_DIMS, preferred_element_type=jnp.float32)
    row_max = jnp.max(scores, axis=-1, keepdims=True)
    weights = jnp.exp2((scores - row_max) * LOG2E).astype(jnp.bfloat16)
    return jnp.dot(weights, value_ones, preferred_element_type=jnp.float32)


def divide_pair(upper, low, high):
    blended = jnp.where(upper, high, low)
    sums = pltpu.roll(jnp.where(upper, low, high), HEAD_DIM, 1)
    return blended / sums


def with_ones(value_pair, half):
    upper = lane_half(value_pair.shape[0])
    own = upper if half else jnp.logical_not(upper)
    return jnp.where(own, value_pair.astype(jnp.float32), 1.0).astype(jnp.bfloat16)


def difference(feature, old):
    change = (feature.astype(jnp.float32) - old.astype(jnp.float32)) / INTERVAL
    return change.astype(jnp.bfloat16)


def spatial_kernel(tile, class_ref, q_ref, k_ref, v_ref, old_ref, *refs):
    out_ref, change_ref, acc_ref = refs[-3:]
    pair = pl.program_id(0)
    positions = q_ref.shape[1]
    upper = lane_half(tile)
    for half in range(2):

        @pl.when(class_ref[2 * pair + half] == 0)
        def _():
            value_ones = with_ones(v_ref[0], half)
            for at in range(0, positions, tile):
                acc_ref[half, pl.ds(at, tile), :] = one_head(
                    q_ref[0, pl.ds(at, tile), :].astype(jnp.float32),
                    upper, half, k_ref[0], value_ones,
                )

    for at in range(0, positions, tile):
        feature = divide_pair(
            upper, acc_ref[0, pl.ds(at, tile), :], acc_ref[1, pl.ds(at, tile), :]
        ).astype(jnp.bfloat16)
        out_ref[0, pl.ds(at, tile), :] = feature
        change_ref[0, pl.ds(at, tile), :] = difference(feature, old_ref[0, pl.ds(at, tile), :])


def spatial_call(frame, classes, queries, key_states, value_states, old_feature, begun=()):
    _, positions, row_width = queries.shape
    pairs = row_width // PAIR
    spec = pl.BlockSpec((1, positions, PAIR), lambda p, c: (frame, 0, p))
    shape = jax.ShapeDtypeStruct(queries.shape, jnp.bfloat16)
    return pl.pallas_call(
        functools.partial(spatial_kernel, 256),
        grid_spec=pltpu.PrefetchScalarGridSpec(
            num_scalar_prefetch=1,
            grid=(pairs,),
            in_specs=[spec] * 4 + [pl.BlockSpec(memory_space=pl.ANY)] * len(begun),
            out_specs=[spec] * 2,
            scratch_shapes=[pltpu.VMEM((2, positions, PAIR), jnp.float32)],
        ),
        out_shape=[shape] * 2,
        input_output_aliases={5 + at: at for at in range(len(begun))},
        compiler_params=params(),
        cost_estimate=pl.CostEstimate(
            flops=2 * pairs * positions * positions * HEAD_DIM * 16,
            bytes_accessed=12 * positions * row_width,
            transcendentals=2 * pairs * positions * positions,
        ),
        name="spatial",
    )(classes, queries, key_states, value_states, old_feature, *begun)


def moved(block, parity):
    wide = block.astype(jnp.float32)
    return jnp.where(parity == 1, pltpu.roll(wide, HEAD_DIM, 1), wide)


def pack_kernel(heads_ref, qa, ka, va, qb, kb, vb, out_ref):
    slot = 2 * pl.program_id(0)
    left_parity = lax.rem(heads_ref[slot], 2)
    right_parity = 1 - lax.rem(heads_ref[slot + 1], 2)
    positions = qa.shape[1]
    upper = lane_half(positions)
    for at, (left, right) in enumerate(((qa, qb), (ka, kb), (va, vb))):
        both = jnp.where(upper, moved(right[0], right_parity), moved(left[0], left_parity))
        out_ref[:, at, 0, 0] = both.astype(jnp.bfloat16).reshape(
            out_ref.shape[0], positions // out_ref.shape[0], PAIR
        )


def pack_call(slot_pairs, sources, heads, tensors):
    frames_dev, positions, _ = tensors[0].shape
    span = positions // sources
    left = pl.BlockSpec((1, positions, PAIR), lambda t, f, h: (f, 0, h[2 * t] // 2))
    right = pl.BlockSpec((1, positions, PAIR), lambda t, f, h: (f, 0, h[2 * t + 1] // 2))
    return pl.pallas_call(
        pack_kernel,
        grid_spec=pltpu.PrefetchScalarGridSpec(
            num_scalar_prefetch=1,
            grid=(slot_pairs, frames_dev),
            in_specs=[left] * 3 + [right] * 3,
            out_specs=pl.BlockSpec(
                (sources, 3, 1, 1, span, PAIR), lambda t, f, h: (0, 0, t, f, 0, 0)
            ),
        ),
        out_shape=jax.ShapeDtypeStruct(
            (sources, 3, slot_pairs, frames_dev, span, PAIR), jnp.bfloat16
        ),
        compiler_params=params(),
        name="pack",
    )(heads, *tensors, *tensors)


def temporal_kernel(list_ref, q_ref, k_ref, v_ref, out_ref, key_ref, value_ref):
    pair = pl.program_id(0)
    groups = pl.num_programs(1)
    group = pl.program_id(1)
    step = q_ref.shape[4] // GROUP
    shape = (q_ref.shape[0], q_ref.shape[3], step, PAIR)
    upper = lane_half(BLOCK)
    for block in range(GROUP):
        rows = pl.ds(block * BLOCK, BLOCK)
        here = pl.ds(block * step, step)
        key_ref[rows, :] = k_ref[:, 0, 0, :, here, :].reshape(BLOCK, PAIR)
        value_tile = v_ref[:, 0, 0, :, here, :].reshape(BLOCK, PAIR)
        for half in range(2):
            value_ref[half, rows, :] = with_ones(value_tile, half)
    for block in range(GROUP):
        here = pl.ds(block * step, step)
        query_tile = q_ref[:, 0, 0, :, here, :].reshape(BLOCK, PAIR).astype(jnp.float32)
        parts = []
        for half in range(2):
            base = (((2 * pair + half) * groups + group) * GROUP + block) * LISTED
            rows = [
                pl.ds(pl.multiple_of(list_ref[base + at] * BLOCK, BLOCK), BLOCK)
                for at in range(LISTED)
            ]
            key_tile = jnp.concatenate([key_ref[row, :] for row in rows], axis=0)
            value_ones = jnp.concatenate([value_ref[half, row, :] for row in rows], axis=0)
            parts.append(one_head(query_tile, upper, half, key_tile, value_ones))
        out_ref[:, 0, :, here, :] = (
            divide_pair(upper, parts[0], parts[1]).astype(jnp.bfloat16).reshape(shape)
        )


def temporal_call(lists, arrived):
    sources, _, slot_pairs, frames_dev, span, _ = arrived.shape
    group_span = GROUP * BLOCK // (sources * frames_dev)
    groups = span // group_span
    size = (sources, 1, 1, frames_dev, group_span, PAIR)

    def spec(tensor):
        return pl.BlockSpec(size, lambda t, g, l: (0, tensor, t, 0, g, 0))

    return pl.pallas_call(
        temporal_kernel,
        grid_spec=pltpu.PrefetchScalarGridSpec(
            num_scalar_prefetch=1,
            grid=(slot_pairs, groups),
            in_specs=[spec(0), spec(1), spec(2)],
            out_specs=pl.BlockSpec(
                (sources, 1, frames_dev, group_span, PAIR), lambda t, g, l: (0, t, 0, g, 0)
            ),
            scratch_shapes=[
                pltpu.VMEM((GROUP * BLOCK, PAIR), jnp.bfloat16),
                pltpu.VMEM((2, GROUP * BLOCK, PAIR), jnp.bfloat16),
            ],
        ),
        out_shape=jax.ShapeDtypeStruct(
            (sources, slot_pairs, frames_dev, span, PAIR), jnp.bfloat16
        ),
        compiler_params=params(),
        name="temporal",
    )(lists, arrived, arrived, arrived)


def merge_kernel(class_ref, slot_ref, visit_ref, spatial_ref, old_ref, _, *refs):
    returned_refs = refs[:-3]
    feature_ref, derivative_ref, held_ref = refs[-3:]
    pair = visit_ref[pl.program_id(1)]
    positions = old_ref.shape[1]
    upper = lane_half(positions)

    @pl.when(pl.program_id(1) == 0)
    def _():
        at = 0
        for returned_ref in returned_refs:
            for own in range(returned_ref.shape[1]):
                held_ref[at] = returned_ref[:, own, 0].reshape(positions, PAIR)
                at += 1

    low_slot = slot_ref[2 * pair]
    high_slot = slot_ref[2 * pair + 1]
    low = moved(held_ref[low_slot // 2], lax.rem(low_slot, 2))
    high = moved(held_ref[high_slot // 2], 1 - lax.rem(high_slot, 2))
    chosen = jnp.where(upper, class_ref[2 * pair + 1], class_ref[2 * pair]) == 1
    kept = jnp.where(chosen, jnp.where(upper, high, low), spatial_ref[0].astype(jnp.float32))
    feature = kept.astype(jnp.bfloat16)
    feature_ref[0] = feature
    derivative_ref[0] = difference(feature, old_ref[0])


def merge_call(classes, slots, visits, feature, derivative, old_feature, returned):
    frames_dev, positions, row_width = feature.shape
    sources, _, _, span, _ = returned[0].shape
    slot_pairs = sum(array.shape[1] for array in returned)
    steps = min(row_width // PAIR, 2 * slot_pairs)
    spec = pl.BlockSpec((1, positions, PAIR), lambda f, p, c, s, v: (f, 0, v[p]))
    arrived = [
        pl.BlockSpec(
            (sources, array.shape[1], 1, span, PAIR), lambda f, p, c, s, v: (0, 0, f, 0, 0)
        )
        for array in returned
    ]
    shape = jax.ShapeDtypeStruct(feature.shape, jnp.bfloat16)
    return pl.pallas_call(
        merge_kernel,
        grid_spec=pltpu.PrefetchScalarGridSpec(
            num_scalar_prefetch=3,
            grid=(frames_dev, steps),
            in_specs=[spec, spec, pl.BlockSpec(memory_space=pl.ANY)] + arrived,
            out_specs=[spec, spec],
            scratch_shapes=[pltpu.VMEM((slot_pairs, positions, PAIR), jnp.bfloat16)],
        ),
        out_shape=(shape, shape),
        input_output_aliases={3: 0, 5: 1},
        compiler_params=params(),
        name="merge",
    )(classes, slots, visits, feature, old_feature, derivative, *returned)


def per_device(queries, key_states, value_states, old_feature, head_class, block_index):
    frames_dev, positions, row_width = queries.shape
    head_count = row_width // HEAD_DIM
    pair_count = lax.axis_size("pair")
    sources = lax.axis_size("frame")
    frames = frames_dev * sources
    span = positions // sources
    group_span = GROUP * BLOCK // frames
    if row_width % PAIR or BLOCK % (frames * 16) or span % group_span:
        return per_device_plain(
            queries, key_states, value_states, old_feature, head_class, block_index
        )
    holder = lax.axis_index("head") * pair_count + lax.axis_index("pair")
    head_start = holder * head_count
    classes = lax.dynamic_slice_in_dim(head_class, head_start, head_count)
    is_temporal = (classes == 1).astype(jnp.int32)
    slots = jnp.where(is_temporal == 1, jnp.cumsum(is_temporal) - 1, 0)
    heads = jnp.sum(
        jnp.where(
            (slots[None, :] == jnp.arange(head_count)[:, None]) & (is_temporal[None, :] == 1),
            jnp.arange(head_count, dtype=jnp.int32)[None, :],
            0,
        ),
        axis=1,
    ).astype(jnp.int32)
    count = jnp.sum(is_temporal)
    groups = span // group_span
    lists = lax.dynamic_slice(
        block_index,
        (head_start, lax.axis_index("frame") * groups * GROUP, 0),
        (head_count, groups * GROUP, LISTED),
    ).reshape(head_count, -1)
    lists = jnp.sum(
        jnp.where(
            heads[:, None, None] == jnp.arange(head_count, dtype=jnp.int32)[None, :, None],
            lists[None],
            0,
        ),
        axis=1,
    )
    pairs = head_count // 2
    pair_used = jnp.max(is_temporal.reshape(pairs, 2), axis=1)
    order = jnp.cumsum(pair_used) - 1
    last = jnp.max(jnp.where(pair_used == 1, jnp.arange(pairs), 0))
    visits = jnp.sum(
        jnp.where(
            (order[None, :] == jnp.arange(pairs)[:, None]) & (pair_used[None, :] == 1),
            jnp.arange(pairs)[None, :],
            0,
        ),
        axis=1,
    )
    visits = jnp.where(jnp.arange(pairs) < jnp.sum(pair_used), visits, last).astype(jnp.int32)
    tensors = (queries, key_states, value_states)

    def exchange(array):
        return lax.all_to_all(array, "frame", split_axis=0, concat_axis=0, tiled=True)

    def none_temporal(tensors, old_feature, classes, slots, visits, heads, lists):
        made = ()
        for frame in range(frames_dev):
            made = spatial_call(frame, classes, *tensors, old_feature, made)
        return tuple(made)

    def some_temporal(slot_pairs):
        def run(tensors, old_feature, classes, slots, visits, heads, lists):
            arrived, temporal = [], []
            made = ()
            beside = [[] for _ in range(slot_pairs + 1)]
            for frame in range(frames_dev):
                beside[min(frame, slot_pairs - 1)].append(frame)
            waited = ()
            for at in range(slot_pairs):
                packed = pack_call(1, sources, heads[2 * at : 2 * at + 2], tensors)
                packed, waited = lax.optimization_barrier((packed, waited))
                got = exchange(packed)
                if at > 0:
                    own_lists = lists[2 * at - 2 : 2 * at].reshape(-1)
                    temporal.append(temporal_call(own_lists, arrived[-1]))
                for frame in beside[at]:
                    made = spatial_call(frame, classes, *tensors, old_feature, made)
                waited = (tuple(temporal), tuple(made))
                got, waited = lax.optimization_barrier((got, waited))
                temporal, made = list(waited[0]), waited[1]
                arrived.append(got)
            returned = []
            if temporal:
                several = exchange(jnp.concatenate(temporal, axis=1))
                final = temporal_call(lists[2 * slot_pairs - 2 : 2 * slot_pairs].reshape(-1), arrived[-1])
                several, final = lax.optimization_barrier((several, final))
                returned.append(several)
            else:
                final = temporal_call(lists[:2].reshape(-1), arrived[-1])
            returned.append(exchange(final))
            return tuple(merge_call(classes, slots, visits, *made, old_feature, returned))

        return run

    branches = [none_temporal] + [some_temporal(n + 1) for n in range((head_count + 1) // 2)]
    return lax.switch(
        (count + 1) // 2, branches,
        tensors, old_feature, is_temporal, slots, visits, heads, lists,
    )


def solution(mesh):
    in_specs = (
        P(("groups", "frame"), None, ("head", "pair")),
        P(("groups", "frame"), None, ("head", "pair")),
        P(("groups", "frame"), None, ("head", "pair")),
        P(("groups", "frame"), None, ("head", "pair")),
        P(),
        P(),
    )
    out_specs = (
        P(("groups", "frame"), None, ("head", "pair")),
        P(("groups", "frame"), None, ("head", "pair")),
    )
    return jax.shard_map(
        per_device, mesh=mesh, in_specs=in_specs, out_specs=out_specs, check_vma=False
    )
```

```python
import functools

import jax
import jax.numpy as jnp
from jax import lax
from jax.experimental import pallas as pl
from jax.experimental.pallas import tpu as pltpu
from jax.sharding import PartitionSpec as P

HEAD_DIM = 64
BLOCK = 128
GROUP = 8
LISTED = 4
INTERVAL = 5


def softmax_read(query_tile, key_tile, value_tile, keep_mask):
    scores = jnp.einsum(
        "...qd,...kd->...qk", query_tile, key_tile, preferred_element_type=jnp.float32
    ) * HEAD_DIM ** (-0.5)
    if keep_mask is not None:
        scores = jnp.where(keep_mask, scores, -jnp.inf)
    row_max = jnp.max(scores, axis=-1, keepdims=True)
    exponent = jnp.exp(scores - row_max)
    row_sum = jnp.sum(exponent, axis=-1, keepdims=True)
    weights = exponent.astype(jnp.bfloat16)
    blended = jnp.einsum(
        "...qk,...kd->...qd", weights, value_tile, preferred_element_type=jnp.float32
    )
    return blended / row_sum


def spatial_part(queries, key_states, value_states, head_count):
    frames_dev, positions, row_width = queries.shape

    def as_items(tensor):
        shaped = tensor.reshape(frames_dev, positions, head_count, HEAD_DIM)
        return shaped.transpose(0, 2, 1, 3).reshape(frames_dev * head_count, positions, HEAD_DIM)

    def spatial_attend_one(pieces):
        return softmax_read(pieces[0], pieces[1], pieces[2], None)

    blended = lax.map(
        spatial_attend_one, (as_items(queries), as_items(key_states), as_items(value_states))
    )
    blended = blended.reshape(frames_dev, head_count, positions, HEAD_DIM).transpose(0, 2, 1, 3)
    return blended.reshape(frames_dev, positions, row_width)


def temporal_part(queries, key_states, value_states, block_lists, head_count):
    frames, local_span, row_width = queries.shape
    group_span = GROUP * BLOCK // frames
    group_count = local_span // group_span

    def as_items(tensor):
        shaped = tensor.reshape(frames, group_count, group_span, head_count, HEAD_DIM)
        return shaped.transpose(1, 3, 0, 2, 4).reshape(
            group_count * head_count, frames * group_span, HEAD_DIM
        )

    listed_all = block_lists.reshape(head_count, group_count, GROUP, LISTED).transpose(1, 0, 2, 3)
    listed_all = listed_all.reshape(group_count * head_count, GROUP, LISTED)
    offsets = jnp.arange(GROUP, dtype=jnp.int32)
    block_of = (
        jnp.arange(group_span, dtype=jnp.int32)[None, :] * frames
        + jnp.arange(frames, dtype=jnp.int32)[:, None]
    ).reshape(-1) // BLOCK
    member = (block_of[:, None] == offsets[None, :]).astype(jnp.float32)

    def temporal_attend_one(pieces):
        query_tile, key_tile, value_tile, listed = pieces
        allowed = jnp.any(listed[:, :, None] == offsets[None, None, :], axis=1).astype(jnp.float32)
        keep_mask = jnp.dot(jnp.dot(member, allowed), member.T) > 0.5
        return softmax_read(query_tile, key_tile, value_tile, keep_mask)

    blended = lax.map(
        temporal_attend_one,
        (as_items(queries), as_items(key_states), as_items(value_states), listed_all),
    )
    blended = blended.reshape(group_count, head_count, frames, group_span, HEAD_DIM).transpose(
        2, 0, 3, 1, 4
    )
    return blended.reshape(frames, local_span, row_width).astype(jnp.bfloat16)


def per_device_plain(queries, key_states, value_states, old_feature, head_class, block_index):
    frames_dev, positions, row_width = queries.shape
    head_count = row_width // HEAD_DIM
    pair_count = lax.axis_size("pair")
    sources = lax.axis_size("frame")
    frames = frames_dev * sources
    group_span = GROUP * BLOCK // frames
    head_start = (lax.axis_index("head") * pair_count + lax.axis_index("pair")) * head_count
    spatial = spatial_part(queries, key_states, value_states, head_count)
    local_span = positions // sources
    arrived = (
        lax.all_to_all(queries, "frame", split_axis=1, concat_axis=0, tiled=True),
        lax.all_to_all(key_states, "frame", split_axis=1, concat_axis=0, tiled=True),
        lax.all_to_all(value_states, "frame", split_axis=1, concat_axis=0, tiled=True),
    )
    first_position = lax.axis_index("frame") * local_span
    block_lists = lax.dynamic_slice(
        block_index,
        (head_start, first_position // group_span * GROUP, 0),
        (head_count, local_span // group_span * GROUP, LISTED),
    )
    temporal = temporal_part(arrived[0], arrived[1], arrived[2], block_lists, head_count)
    returned = lax.all_to_all(temporal, "frame", split_axis=0, concat_axis=1, tiled=True)
    column_class = jnp.repeat(
        lax.dynamic_slice_in_dim(head_class, head_start, head_count), HEAD_DIM
    )
    feature = jnp.where(column_class[None, None, :] == 1, returned, spatial.astype(jnp.bfloat16))
    kept = lax.optimization_barrier(feature).astype(jnp.float32)
    derivative = ((kept - old_feature.astype(jnp.float32)) / INTERVAL).astype(jnp.bfloat16)
    return (feature, derivative)


PAIR = 2 * HEAD_DIM
LOG2E = 1.4426950408889634
NT_DIMS = (((1,), (1,)), ((), ()))


def params():
    return pltpu.CompilerParams(vmem_limit_bytes=40 * 1024 * 1024)


def lane_half(rows):
    return lax.broadcasted_iota(jnp.int32, (rows, PAIR), 1) >= HEAD_DIM


def one_head(query_pair, upper, half, key_tile, value_ones):
    own = upper if half else jnp.logical_not(upper)
    scaled = jnp.where(own, query_pair * HEAD_DIM ** (-0.5), 0.0).astype(jnp.bfloat16)
    scores = lax.dot_general(scaled, key_tile, NT_DIMS, preferred_element_type=jnp.float32)
    row_max = jnp.max(scores, axis=-1, keepdims=True)
    weights = jnp.exp2((scores - row_max) * LOG2E).astype(jnp.bfloat16)
    return jnp.dot(weights, value_ones, preferred_element_type=jnp.float32)


def divide_pair(upper, low, high):
    blended = jnp.where(upper, high, low)
    sums = pltpu.roll(jnp.where(upper, low, high), HEAD_DIM, 1)
    return blended / sums


def with_ones(value_pair, half):
    upper = lane_half(value_pair.shape[0])
    own = upper if half else jnp.logical_not(upper)
    return jnp.where(own, value_pair.astype(jnp.float32), 1.0).astype(jnp.bfloat16)


def difference(feature, old):
    change = (feature.astype(jnp.float32) - old.astype(jnp.float32)) / INTERVAL
    return change.astype(jnp.bfloat16)


def spatial_kernel(tile, class_ref, q_ref, k_ref, v_ref, old_ref, *refs):
    out_ref, change_ref, acc_ref = refs[-3:]
    pair = pl.program_id(0)
    positions = q_ref.shape[1]
    upper = lane_half(tile)
    for half in range(2):

        @pl.when(class_ref[2 * pair + half] == 0)
        def _():
            value_ones = with_ones(v_ref[0], half)

            @pl.loop(0, positions // tile)
            def _(at):
                rows = pl.ds(pl.multiple_of(at * tile, tile), tile)
                acc_ref[half, rows, :] = one_head(
                    q_ref[0, rows, :].astype(jnp.float32), upper, half, k_ref[0], value_ones
                )

    @pl.loop(0, positions // tile)
    def _(at):
        rows = pl.ds(pl.multiple_of(at * tile, tile), tile)
        feature = divide_pair(upper, acc_ref[0, rows, :], acc_ref[1, rows, :]).astype(jnp.bfloat16)
        out_ref[0, rows, :] = feature
        change_ref[0, rows, :] = difference(feature, old_ref[0, rows, :])


def spatial_call(frame, classes, queries, key_states, value_states, old_feature, begun=()):
    _, positions, row_width = queries.shape
    pairs = row_width // PAIR
    spec = pl.BlockSpec((1, positions, PAIR), lambda p, c: (frame, 0, p))
    shape = jax.ShapeDtypeStruct(queries.shape, jnp.bfloat16)
    return pl.pallas_call(
        functools.partial(spatial_kernel, 256),
        grid_spec=pltpu.PrefetchScalarGridSpec(
            num_scalar_prefetch=1,
            grid=(pairs,),
            in_specs=[spec] * 4 + [pl.BlockSpec(memory_space=pl.ANY)] * len(begun),
            out_specs=[spec] * 2,
            scratch_shapes=[pltpu.VMEM((2, positions, PAIR), jnp.float32)],
        ),
        out_shape=[shape] * 2,
        input_output_aliases={5 + at: at for at in range(len(begun))},
        compiler_params=params(),
        cost_estimate=pl.CostEstimate(
            flops=2 * pairs * positions * positions * HEAD_DIM * 16,
            bytes_accessed=12 * positions * row_width,
            transcendentals=2 * pairs * positions * positions,
        ),
        name="spatial",
    )(classes, queries, key_states, value_states, old_feature, *begun)


def moved(block, parity):
    wide = block.astype(jnp.float32)
    return jnp.where(parity == 1, pltpu.roll(wide, HEAD_DIM, 1), wide)


def pack_kernel(heads_ref, qa, ka, va, qb, kb, vb, out_ref):
    slot = 2 * pl.program_id(0)
    left_parity = lax.rem(heads_ref[slot], 2)
    right_parity = 1 - lax.rem(heads_ref[slot + 1], 2)
    positions = qa.shape[1]
    span = positions // out_ref.shape[0]
    upper = lane_half(span)

    @pl.loop(0, out_ref.shape[0])
    def _(source):
        rows = pl.ds(pl.multiple_of(source * span, span), span)
        for at, (left, right) in enumerate(((qa, qb), (ka, kb), (va, vb))):
            both = jnp.where(
                upper, moved(right[0, rows, :], right_parity), moved(left[0, rows, :], left_parity)
            )
            out_ref[source, at, 0, 0] = both.astype(jnp.bfloat16)


def pack_call(slot_pairs, sources, heads, tensors):
    frames_dev, positions, _ = tensors[0].shape
    span = positions // sources
    left = pl.BlockSpec((1, positions, PAIR), lambda t, f, h: (f, 0, h[2 * t] // 2))
    right = pl.BlockSpec((1, positions, PAIR), lambda t, f, h: (f, 0, h[2 * t + 1] // 2))
    return pl.pallas_call(
        pack_kernel,
        grid_spec=pltpu.PrefetchScalarGridSpec(
            num_scalar_prefetch=1,
            grid=(slot_pairs, frames_dev),
            in_specs=[left] * 3 + [right] * 3,
            out_specs=pl.BlockSpec(
                (sources, 3, 1, 1, span, PAIR), lambda t, f, h: (0, 0, t, f, 0, 0)
            ),
        ),
        out_shape=jax.ShapeDtypeStruct(
            (sources, 3, slot_pairs, frames_dev, span, PAIR), jnp.bfloat16
        ),
        compiler_params=params(),
        name="pack",
    )(heads, *tensors, *tensors)


def temporal_kernel(list_ref, q_ref, k_ref, v_ref, out_ref, key_ref, value_ref):
    pair = pl.program_id(0)
    groups = pl.num_programs(1)
    group = pl.program_id(1)
    step = q_ref.shape[4] // GROUP
    shape = (q_ref.shape[0], q_ref.shape[3], step, PAIR)
    upper = lane_half(BLOCK)

    @pl.loop(0, GROUP)
    def _(block):
        rows = pl.ds(pl.multiple_of(block * BLOCK, BLOCK), BLOCK)
        here = pl.ds(pl.multiple_of(block * step, step), step)
        key_ref[rows, :] = k_ref[:, 0, 0, :, here, :].reshape(BLOCK, PAIR)
        value_tile = v_ref[:, 0, 0, :, here, :].reshape(BLOCK, PAIR)
        for half in range(2):
            value_ref[half, rows, :] = with_ones(value_tile, half)

    @pl.loop(0, GROUP)
    def _(block):
        here = pl.ds(pl.multiple_of(block * step, step), step)
        query_tile = q_ref[:, 0, 0, :, here, :].reshape(BLOCK, PAIR).astype(jnp.float32)
        parts = []
        for half in range(2):
            base = (((2 * pair + half) * groups + group) * GROUP + block) * LISTED
            rows = [
                pl.ds(pl.multiple_of(list_ref[base + at] * BLOCK, BLOCK), BLOCK)
                for at in range(LISTED)
            ]
            key_tile = jnp.concatenate([key_ref[row, :] for row in rows], axis=0)
            value_ones = jnp.concatenate([value_ref[half, row, :] for row in rows], axis=0)
            parts.append(one_head(query_tile, upper, half, key_tile, value_ones))
        out_ref[:, 0, :, here, :] = (
            divide_pair(upper, parts[0], parts[1]).astype(jnp.bfloat16).reshape(shape)
        )


def temporal_call(lists, arrived):
    sources, _, slot_pairs, frames_dev, span, _ = arrived.shape
    group_span = GROUP * BLOCK // (sources * frames_dev)
    groups = span // group_span
    size = (sources, 1, 1, frames_dev, group_span, PAIR)

    def spec(tensor):
        return pl.BlockSpec(size, lambda t, g, l: (0, tensor, t, 0, g, 0))

    return pl.pallas_call(
        temporal_kernel,
        grid_spec=pltpu.PrefetchScalarGridSpec(
            num_scalar_prefetch=1,
            grid=(slot_pairs, groups),
            in_specs=[spec(0), spec(1), spec(2)],
            out_specs=pl.BlockSpec(
                (sources, 1, frames_dev, group_span, PAIR), lambda t, g, l: (0, t, 0, g, 0)
            ),
            scratch_shapes=[
                pltpu.VMEM((GROUP * BLOCK, PAIR), jnp.bfloat16),
                pltpu.VMEM((2, GROUP * BLOCK, PAIR), jnp.bfloat16),
            ],
        ),
        out_shape=jax.ShapeDtypeStruct(
            (sources, slot_pairs, frames_dev, span, PAIR), jnp.bfloat16
        ),
        compiler_params=params(),
        name="temporal",
    )(lists, arrived, arrived, arrived)


def merge_kernel(class_ref, slot_ref, visit_ref, spatial_ref, old_ref, _, *refs):
    returned_refs = refs[:-3]
    feature_ref, derivative_ref, held_ref = refs[-3:]
    pair = visit_ref[pl.program_id(1)]
    sources, _, _, span, _ = returned_refs[0].shape
    upper = lane_half(span)

    @pl.when(pl.program_id(1) == 0)
    def _():
        @pl.loop(0, sources)
        def _(source):
            at = 0
            for returned_ref in returned_refs:
                for own in range(returned_ref.shape[1]):
                    held_ref[at, source] = returned_ref[source, own, 0]
                    at += 1

    low_slot = slot_ref[2 * pair]
    high_slot = slot_ref[2 * pair + 1]
    chosen = jnp.where(upper, class_ref[2 * pair + 1], class_ref[2 * pair]) == 1

    @pl.loop(0, sources)
    def _(source):
        rows = pl.ds(pl.multiple_of(source * span, span), span)
        low = moved(held_ref[low_slot // 2, source], lax.rem(low_slot, 2))
        high = moved(held_ref[high_slot // 2, source], 1 - lax.rem(high_slot, 2))
        own = spatial_ref[0, rows, :].astype(jnp.float32)
        feature = jnp.where(chosen, jnp.where(upper, high, low), own).astype(jnp.bfloat16)
        feature_ref[0, rows, :] = feature
        derivative_ref[0, rows, :] = difference(feature, old_ref[0, rows, :])


def merge_call(classes, slots, visits, feature, derivative, old_feature, returned):
    frames_dev, positions, row_width = feature.shape
    sources, _, _, span, _ = returned[0].shape
    slot_pairs = sum(array.shape[1] for array in returned)
    steps = min(row_width // PAIR, 2 * slot_pairs)
    spec = pl.BlockSpec((1, positions, PAIR), lambda f, p, c, s, v: (f, 0, v[p]))
    arrived = [
        pl.BlockSpec(
            (sources, array.shape[1], 1, span, PAIR), lambda f, p, c, s, v: (0, 0, f, 0, 0)
        )
        for array in returned
    ]
    shape = jax.ShapeDtypeStruct(feature.shape, jnp.bfloat16)
    return pl.pallas_call(
        merge_kernel,
        grid_spec=pltpu.PrefetchScalarGridSpec(
            num_scalar_prefetch=3,
            grid=(frames_dev, steps),
            in_specs=[spec, spec, pl.BlockSpec(memory_space=pl.ANY)] + arrived,
            out_specs=[spec, spec],
            scratch_shapes=[pltpu.VMEM((slot_pairs, sources, span, PAIR), jnp.bfloat16)],
        ),
        out_shape=(shape, shape),
        input_output_aliases={3: 0, 5: 1},
        compiler_params=params(),
        name="merge",
    )(classes, slots, visits, feature, old_feature, derivative, *returned)


def per_device(queries, key_states, value_states, old_feature, head_class, block_index):
    frames_dev, positions, row_width = queries.shape
    head_count = row_width // HEAD_DIM
    pair_count = lax.axis_size("pair")
    sources = lax.axis_size("frame")
    frames = frames_dev * sources
    span = positions // sources
    group_span = GROUP * BLOCK // frames
    if row_width % PAIR or BLOCK % (frames * 16) or span % group_span:
        return per_device_plain(
            queries, key_states, value_states, old_feature, head_class, block_index
        )
    holder = lax.axis_index("head") * pair_count + lax.axis_index("pair")
    head_start = holder * head_count
    classes = lax.dynamic_slice_in_dim(head_class, head_start, head_count)
    is_temporal = (classes == 1).astype(jnp.int32)
    slots = jnp.where(is_temporal == 1, jnp.cumsum(is_temporal) - 1, 0)
    heads = jnp.sum(
        jnp.where(
            (slots[None, :] == jnp.arange(head_count)[:, None]) & (is_temporal[None, :] == 1),
            jnp.arange(head_count, dtype=jnp.int32)[None, :],
            0,
        ),
        axis=1,
    ).astype(jnp.int32)
    count = jnp.sum(is_temporal)
    groups = span // group_span
    lists = lax.dynamic_slice(
        block_index,
        (head_start, lax.axis_index("frame") * groups * GROUP, 0),
        (head_count, groups * GROUP, LISTED),
    ).reshape(head_count, -1)
    lists = jnp.sum(
        jnp.where(
            heads[:, None, None] == jnp.arange(head_count, dtype=jnp.int32)[None, :, None],
            lists[None],
            0,
        ),
        axis=1,
    )
    pairs = head_count // 2
    pair_used = jnp.max(is_temporal.reshape(pairs, 2), axis=1)
    order = jnp.cumsum(pair_used) - 1
    last = jnp.max(jnp.where(pair_used == 1, jnp.arange(pairs), 0))
    visits = jnp.sum(
        jnp.where(
            (order[None, :] == jnp.arange(pairs)[:, None]) & (pair_used[None, :] == 1),
            jnp.arange(pairs)[None, :],
            0,
        ),
        axis=1,
    )
    visits = jnp.where(jnp.arange(pairs) < jnp.sum(pair_used), visits, last).astype(jnp.int32)
    tensors = (queries, key_states, value_states)

    def exchange(array):
        return lax.all_to_all(array, "frame", split_axis=0, concat_axis=0, tiled=True)

    def none_temporal(tensors, old_feature, classes, slots, visits, heads, lists):
        made = ()
        for frame in range(frames_dev):
            made = spatial_call(frame, classes, *tensors, old_feature, made)
        return tuple(made)

    def some_temporal(slot_pairs):
        def run(tensors, old_feature, classes, slots, visits, heads, lists):
            arrived, temporal = [], []
            made = ()
            beside = [[] for _ in range(slot_pairs + 1)]
            for frame in range(frames_dev):
                beside[min(frame, slot_pairs - 1)].append(frame)
            waited = ()
            for at in range(slot_pairs):
                packed = pack_call(1, sources, heads[2 * at : 2 * at + 2], tensors)
                packed, waited = lax.optimization_barrier((packed, waited))
                got = exchange(packed)
                if at > 0:
                    own_lists = lists[2 * at - 2 : 2 * at].reshape(-1)
                    temporal.append(temporal_call(own_lists, arrived[-1]))
                for frame in beside[at]:
                    made = spatial_call(frame, classes, *tensors, old_feature, made)
                waited = (tuple(temporal), tuple(made))
                got, waited = lax.optimization_barrier((got, waited))
                temporal, made = list(waited[0]), waited[1]
                arrived.append(got)
            returned = []
            if temporal:
                several = exchange(jnp.concatenate(temporal, axis=1))
                final = temporal_call(lists[2 * slot_pairs - 2 : 2 * slot_pairs].reshape(-1), arrived[-1])
                several, final = lax.optimization_barrier((several, final))
                returned.append(several)
            else:
                final = temporal_call(lists[:2].reshape(-1), arrived[-1])
            returned.append(exchange(final))
            return tuple(merge_call(classes, slots, visits, *made, old_feature, returned))

        return run

    branches = [none_temporal] + [some_temporal(n + 1) for n in range((head_count + 1) // 2)]
    return lax.switch(
        (count + 1) // 2, branches,
        tensors, old_feature, is_temporal, slots, visits, heads, lists,
    )


def solution(mesh):
    in_specs = (
        P(("groups", "frame"), None, ("head", "pair")),
        P(("groups", "frame"), None, ("head", "pair")),
        P(("groups", "frame"), None, ("head", "pair")),
        P(("groups", "frame"), None, ("head", "pair")),
        P(),
        P(),
    )
    out_specs = (
        P(("groups", "frame"), None, ("head", "pair")),
        P(("groups", "frame"), None, ("head", "pair")),
    )
    return jax.shard_map(
        per_device, mesh=mesh, in_specs=in_specs, out_specs=out_specs, check_vma=False
    )
```

```python
import functools

import jax
import jax.numpy as jnp
from jax import lax
from jax.experimental import pallas as pl
from jax.experimental.pallas import tpu as pltpu
from jax.sharding import PartitionSpec as P

HEAD_DIM = 64
BLOCK = 128
GROUP = 8
LISTED = 4
INTERVAL = 5


def softmax_read(query_tile, key_tile, value_tile, keep_mask):
    scores = jnp.einsum(
        "...qd,...kd->...qk", query_tile, key_tile, preferred_element_type=jnp.float32
    ) * HEAD_DIM ** (-0.5)
    if keep_mask is not None:
        scores = jnp.where(keep_mask, scores, -jnp.inf)
    row_max = jnp.max(scores, axis=-1, keepdims=True)
    exponent = jnp.exp(scores - row_max)
    row_sum = jnp.sum(exponent, axis=-1, keepdims=True)
    weights = exponent.astype(jnp.bfloat16)
    blended = jnp.einsum(
        "...qk,...kd->...qd", weights, value_tile, preferred_element_type=jnp.float32
    )
    return blended / row_sum


def spatial_part(queries, key_states, value_states, head_count):
    frames_dev, positions, row_width = queries.shape

    def as_items(tensor):
        shaped = tensor.reshape(frames_dev, positions, head_count, HEAD_DIM)
        return shaped.transpose(0, 2, 1, 3).reshape(frames_dev * head_count, positions, HEAD_DIM)

    def spatial_attend_one(pieces):
        return softmax_read(pieces[0], pieces[1], pieces[2], None)

    blended = lax.map(
        spatial_attend_one, (as_items(queries), as_items(key_states), as_items(value_states))
    )
    blended = blended.reshape(frames_dev, head_count, positions, HEAD_DIM).transpose(0, 2, 1, 3)
    return blended.reshape(frames_dev, positions, row_width)


def temporal_part(queries, key_states, value_states, block_lists, head_count):
    frames, local_span, row_width = queries.shape
    group_span = GROUP * BLOCK // frames
    group_count = local_span // group_span

    def as_items(tensor):
        shaped = tensor.reshape(frames, group_count, group_span, head_count, HEAD_DIM)
        return shaped.transpose(1, 3, 0, 2, 4).reshape(
            group_count * head_count, frames * group_span, HEAD_DIM
        )

    listed_all = block_lists.reshape(head_count, group_count, GROUP, LISTED).transpose(1, 0, 2, 3)
    listed_all = listed_all.reshape(group_count * head_count, GROUP, LISTED)
    offsets = jnp.arange(GROUP, dtype=jnp.int32)
    block_of = (
        jnp.arange(group_span, dtype=jnp.int32)[None, :] * frames
        + jnp.arange(frames, dtype=jnp.int32)[:, None]
    ).reshape(-1) // BLOCK
    member = (block_of[:, None] == offsets[None, :]).astype(jnp.float32)

    def temporal_attend_one(pieces):
        query_tile, key_tile, value_tile, listed = pieces
        allowed = jnp.any(listed[:, :, None] == offsets[None, None, :], axis=1).astype(jnp.float32)
        keep_mask = jnp.dot(jnp.dot(member, allowed), member.T) > 0.5
        return softmax_read(query_tile, key_tile, value_tile, keep_mask)

    blended = lax.map(
        temporal_attend_one,
        (as_items(queries), as_items(key_states), as_items(value_states), listed_all),
    )
    blended = blended.reshape(group_count, head_count, frames, group_span, HEAD_DIM).transpose(
        2, 0, 3, 1, 4
    )
    return blended.reshape(frames, local_span, row_width).astype(jnp.bfloat16)


def per_device_plain(queries, key_states, value_states, old_feature, head_class, block_index):
    frames_dev, positions, row_width = queries.shape
    head_count = row_width // HEAD_DIM
    pair_count = lax.axis_size("pair")
    sources = lax.axis_size("frame")
    frames = frames_dev * sources
    group_span = GROUP * BLOCK // frames
    head_start = (lax.axis_index("head") * pair_count + lax.axis_index("pair")) * head_count
    spatial = spatial_part(queries, key_states, value_states, head_count)
    local_span = positions // sources
    arrived = (
        lax.all_to_all(queries, "frame", split_axis=1, concat_axis=0, tiled=True),
        lax.all_to_all(key_states, "frame", split_axis=1, concat_axis=0, tiled=True),
        lax.all_to_all(value_states, "frame", split_axis=1, concat_axis=0, tiled=True),
    )
    first_position = lax.axis_index("frame") * local_span
    block_lists = lax.dynamic_slice(
        block_index,
        (head_start, first_position // group_span * GROUP, 0),
        (head_count, local_span // group_span * GROUP, LISTED),
    )
    temporal = temporal_part(arrived[0], arrived[1], arrived[2], block_lists, head_count)
    returned = lax.all_to_all(temporal, "frame", split_axis=0, concat_axis=1, tiled=True)
    column_class = jnp.repeat(
        lax.dynamic_slice_in_dim(head_class, head_start, head_count), HEAD_DIM
    )
    feature = jnp.where(column_class[None, None, :] == 1, returned, spatial.astype(jnp.bfloat16))
    kept = lax.optimization_barrier(feature).astype(jnp.float32)
    derivative = ((kept - old_feature.astype(jnp.float32)) / INTERVAL).astype(jnp.bfloat16)
    return (feature, derivative)


PAIR = 2 * HEAD_DIM
LOG2E = 1.4426950408889634
NT_DIMS = (((1,), (1,)), ((), ()))


def params():
    return pltpu.CompilerParams(vmem_limit_bytes=40 * 1024 * 1024)


def lane_half(rows):
    return lax.broadcasted_iota(jnp.int32, (rows, PAIR), 1) >= HEAD_DIM


def one_head(query_pair, upper, half, key_tile, value_ones):
    own = upper if half else jnp.logical_not(upper)
    scaled = jnp.where(own, query_pair * HEAD_DIM ** (-0.5), 0.0).astype(jnp.bfloat16)
    scores = lax.dot_general(scaled, key_tile, NT_DIMS, preferred_element_type=jnp.float32)
    row_max = jnp.max(scores, axis=-1, keepdims=True)
    weights = jnp.exp2((scores - row_max) * LOG2E).astype(jnp.bfloat16)
    return jnp.dot(weights, value_ones, preferred_element_type=jnp.float32)


def divide_pair(upper, low, high):
    blended = jnp.where(upper, high, low)
    sums = pltpu.roll(jnp.where(upper, low, high), HEAD_DIM, 1)
    return blended / sums


def with_ones(value_pair, half):
    upper = lane_half(value_pair.shape[0])
    own = upper if half else jnp.logical_not(upper)
    return jnp.where(own, value_pair.astype(jnp.float32), 1.0).astype(jnp.bfloat16)


def difference(feature, old):
    change = (feature.astype(jnp.float32) - old.astype(jnp.float32)) / INTERVAL
    return change.astype(jnp.bfloat16)


def spatial_kernel(tile, class_ref, q_ref, k_ref, v_ref, old_ref, *refs):
    out_ref, change_ref, acc_ref = refs[-3:]
    pair = pl.program_id(0)
    positions = q_ref.shape[1]
    upper = lane_half(tile)
    for half in range(2):

        @pl.when(class_ref[2 * pair + half] == 0)
        def _():
            value_ones = with_ones(v_ref[0], half)

            @pl.loop(0, positions // tile)
            def _(at):
                rows = pl.ds(pl.multiple_of(at * tile, tile), tile)
                acc_ref[half, rows, :] = one_head(
                    q_ref[0, rows, :].astype(jnp.float32), upper, half, k_ref[0], value_ones
                )

    @pl.loop(0, positions // tile)
    def _(at):
        rows = pl.ds(pl.multiple_of(at * tile, tile), tile)
        feature = divide_pair(upper, acc_ref[0, rows, :], acc_ref[1, rows, :]).astype(jnp.bfloat16)
        out_ref[0, rows, :] = feature
        change_ref[0, rows, :] = difference(feature, old_ref[0, rows, :])


def spatial_call(frame, classes, queries, key_states, value_states, old_feature, begun=()):
    _, positions, row_width = queries.shape
    pairs = row_width // PAIR
    spec = pl.BlockSpec((1, positions, PAIR), lambda p, c: (frame, 0, p))
    shape = jax.ShapeDtypeStruct(queries.shape, jnp.bfloat16)
    return pl.pallas_call(
        functools.partial(spatial_kernel, 256),
        grid_spec=pltpu.PrefetchScalarGridSpec(
            num_scalar_prefetch=1,
            grid=(pairs,),
            in_specs=[spec] * 4 + [pl.BlockSpec(memory_space=pl.ANY)] * len(begun),
            out_specs=[spec] * 2,
            scratch_shapes=[pltpu.VMEM((2, positions, PAIR), jnp.float32)],
        ),
        out_shape=[shape] * 2,
        input_output_aliases={5 + at: at for at in range(len(begun))},
        compiler_params=params(),
        cost_estimate=pl.CostEstimate(
            flops=2 * pairs * positions * positions * HEAD_DIM * 16,
            bytes_accessed=12 * positions * row_width,
            transcendentals=2 * pairs * positions * positions,
        ),
        name="spatial",
    )(classes, queries, key_states, value_states, old_feature, *begun)


def moved(block, parity):
    wide = block.astype(jnp.float32)
    return jnp.where(parity == 1, pltpu.roll(wide, HEAD_DIM, 1), wide)


def pack_kernel(heads_ref, qa, ka, va, qb, kb, vb, out_ref):
    slot = 2 * pl.program_id(0)
    left_parity = lax.rem(heads_ref[slot], 2)
    right_parity = 1 - lax.rem(heads_ref[slot + 1], 2)
    positions = qa.shape[1]
    span = positions // out_ref.shape[0]
    upper = lane_half(span)

    @pl.loop(0, out_ref.shape[0])
    def _(source):
        rows = pl.ds(pl.multiple_of(source * span, span), span)
        for at, (left, right) in enumerate(((qa, qb), (ka, kb), (va, vb))):
            both = jnp.where(
                upper, moved(right[0, rows, :], right_parity), moved(left[0, rows, :], left_parity)
            )
            out_ref[source, at, 0, 0] = both.astype(jnp.bfloat16)


def pack_call(slot_pairs, sources, heads, tensors):
    frames_dev, positions, _ = tensors[0].shape
    span = positions // sources
    left = pl.BlockSpec((1, positions, PAIR), lambda t, f, h: (f, 0, h[2 * t] // 2))
    right = pl.BlockSpec((1, positions, PAIR), lambda t, f, h: (f, 0, h[2 * t + 1] // 2))
    return pl.pallas_call(
        pack_kernel,
        grid_spec=pltpu.PrefetchScalarGridSpec(
            num_scalar_prefetch=1,
            grid=(slot_pairs, frames_dev),
            in_specs=[left] * 3 + [right] * 3,
            out_specs=pl.BlockSpec(
                (sources, 3, 1, 1, span, PAIR), lambda t, f, h: (0, 0, t, f, 0, 0)
            ),
        ),
        out_shape=jax.ShapeDtypeStruct(
            (sources, 3, slot_pairs, frames_dev, span, PAIR), jnp.bfloat16
        ),
        compiler_params=params(),
        name="pack",
    )(heads, *tensors, *tensors)


def temporal_kernel(list_ref, q_ref, k_ref, v_ref, *refs):
    out_ref, key_ref, value_ref = refs[-3:]
    pair = pl.program_id(0)
    groups = pl.num_programs(1)
    group = pl.program_id(1)
    step = q_ref.shape[4] // GROUP
    shape = (q_ref.shape[0], q_ref.shape[3], step, PAIR)
    upper = lane_half(BLOCK)

    @pl.loop(0, GROUP)
    def _(block):
        rows = pl.ds(pl.multiple_of(block * BLOCK, BLOCK), BLOCK)
        here = pl.ds(pl.multiple_of(block * step, step), step)
        key_ref[rows, :] = k_ref[:, 0, 0, :, here, :].reshape(BLOCK, PAIR)
        value_tile = v_ref[:, 0, 0, :, here, :].reshape(BLOCK, PAIR)
        for half in range(2):
            value_ref[half, rows, :] = with_ones(value_tile, half)

    @pl.loop(0, GROUP)
    def _(block):
        here = pl.ds(pl.multiple_of(block * step, step), step)
        query_tile = q_ref[:, 0, 0, :, here, :].reshape(BLOCK, PAIR).astype(jnp.float32)
        parts = []
        for half in range(2):
            base = (((2 * pair + half) * groups + group) * GROUP + block) * LISTED
            rows = [
                pl.ds(pl.multiple_of(list_ref[base + at] * BLOCK, BLOCK), BLOCK)
                for at in range(LISTED)
            ]
            key_tile = jnp.concatenate([key_ref[row, :] for row in rows], axis=0)
            value_ones = jnp.concatenate([value_ref[half, row, :] for row in rows], axis=0)
            parts.append(one_head(query_tile, upper, half, key_tile, value_ones))
        out_ref[:, 0, :, here, :] = (
            divide_pair(upper, parts[0], parts[1]).astype(jnp.bfloat16).reshape(shape)
        )


def temporal_call(lists, arrived, total=1, place=0, begun=()):
    sources, _, slot_pairs, frames_dev, span, _ = arrived.shape
    group_span = GROUP * BLOCK // (sources * frames_dev)
    groups = span // group_span
    size = (sources, 1, 1, frames_dev, group_span, PAIR)

    def spec(tensor):
        return pl.BlockSpec(size, lambda t, g, l: (0, tensor, t, 0, g, 0))

    return pl.pallas_call(
        temporal_kernel,
        grid_spec=pltpu.PrefetchScalarGridSpec(
            num_scalar_prefetch=1,
            grid=(slot_pairs, groups),
            in_specs=[spec(0), spec(1), spec(2)]
            + [pl.BlockSpec(memory_space=pl.ANY)] * len(begun),
            out_specs=pl.BlockSpec(
                (sources, 1, frames_dev, group_span, PAIR), lambda t, g, l: (0, place + t, 0, g, 0)
            ),
            scratch_shapes=[
                pltpu.VMEM((GROUP * BLOCK, PAIR), jnp.bfloat16),
                pltpu.VMEM((2, GROUP * BLOCK, PAIR), jnp.bfloat16),
            ],
        ),
        out_shape=jax.ShapeDtypeStruct(
            (sources, total, frames_dev, span, PAIR), jnp.bfloat16
        ),
        input_output_aliases={4 + at: at for at in range(len(begun))},
        compiler_params=params(),
        name="temporal",
    )(lists, arrived, arrived, arrived, *begun)


def merge_kernel(class_ref, slot_ref, visit_ref, spatial_ref, old_ref, _, *refs):
    returned_refs = refs[:-3]
    feature_ref, derivative_ref, held_ref = refs[-3:]
    pair = visit_ref[pl.program_id(1)]
    sources, _, _, span, _ = returned_refs[0].shape
    upper = lane_half(span)

    @pl.when(pl.program_id(1) == 0)
    def _():
        @pl.loop(0, sources)
        def _(source):
            at = 0
            for returned_ref in returned_refs:
                for own in range(returned_ref.shape[1]):
                    held_ref[at, source] = returned_ref[source, own, 0]
                    at += 1

    low_slot = slot_ref[2 * pair]
    high_slot = slot_ref[2 * pair + 1]
    chosen = jnp.where(upper, class_ref[2 * pair + 1], class_ref[2 * pair]) == 1

    step = pl.program_id(1)
    fresh = (step == 0) | (pair != visit_ref[jnp.maximum(step - 1, 0)])

    @pl.loop(0, jnp.where(fresh, sources, 0))
    def _(source):
        rows = pl.ds(pl.multiple_of(source * span, span), span)
        low = moved(held_ref[low_slot // 2, source], lax.rem(low_slot, 2))
        high = moved(held_ref[high_slot // 2, source], 1 - lax.rem(high_slot, 2))
        own = spatial_ref[0, rows, :].astype(jnp.float32)
        feature = jnp.where(chosen, jnp.where(upper, high, low), own).astype(jnp.bfloat16)
        feature_ref[0, rows, :] = feature
        derivative_ref[0, rows, :] = difference(feature, old_ref[0, rows, :])


def merge_call(classes, slots, visits, feature, derivative, old_feature, returned):
    frames_dev, positions, row_width = feature.shape
    sources, _, _, span, _ = returned[0].shape
    slot_pairs = sum(array.shape[1] for array in returned)
    steps = min(row_width // PAIR, 2 * slot_pairs)
    spec = pl.BlockSpec((1, positions, PAIR), lambda f, p, c, s, v: (f, 0, v[p]))
    arrived = [
        pl.BlockSpec(
            (sources, array.shape[1], 1, span, PAIR), lambda f, p, c, s, v: (0, 0, f, 0, 0)
        )
        for array in returned
    ]
    shape = jax.ShapeDtypeStruct(feature.shape, jnp.bfloat16)
    return pl.pallas_call(
        merge_kernel,
        grid_spec=pltpu.PrefetchScalarGridSpec(
            num_scalar_prefetch=3,
            grid=(frames_dev, steps),
            in_specs=[spec, spec, pl.BlockSpec(memory_space=pl.ANY)] + arrived,
            out_specs=[spec, spec],
            scratch_shapes=[pltpu.VMEM((slot_pairs, sources, span, PAIR), jnp.bfloat16)],
        ),
        out_shape=(shape, shape),
        input_output_aliases={3: 0, 5: 1},
        compiler_params=params(),
        name="merge",
    )(classes, slots, visits, feature, old_feature, derivative, *returned)


def per_device(queries, key_states, value_states, old_feature, head_class, block_index):
    frames_dev, positions, row_width = queries.shape
    head_count = row_width // HEAD_DIM
    pair_count = lax.axis_size("pair")
    sources = lax.axis_size("frame")
    frames = frames_dev * sources
    span = positions // sources
    group_span = GROUP * BLOCK // frames
    if row_width % PAIR or BLOCK % (frames * 16) or span % group_span:
        return per_device_plain(
            queries, key_states, value_states, old_feature, head_class, block_index
        )
    holder = lax.axis_index("head") * pair_count + lax.axis_index("pair")
    head_start = holder * head_count
    classes = lax.dynamic_slice_in_dim(head_class, head_start, head_count)
    is_temporal = (classes == 1).astype(jnp.int32)
    slots = jnp.where(is_temporal == 1, jnp.cumsum(is_temporal) - 1, 0)
    heads = jnp.sum(
        jnp.where(
            (slots[None, :] == jnp.arange(head_count)[:, None]) & (is_temporal[None, :] == 1),
            jnp.arange(head_count, dtype=jnp.int32)[None, :],
            0,
        ),
        axis=1,
    ).astype(jnp.int32)
    count = jnp.sum(is_temporal)
    groups = span // group_span
    lists = lax.dynamic_slice(
        block_index,
        (head_start, lax.axis_index("frame") * groups * GROUP, 0),
        (head_count, groups * GROUP, LISTED),
    ).reshape(head_count, -1)
    lists = jnp.sum(
        jnp.where(
            heads[:, None, None] == jnp.arange(head_count, dtype=jnp.int32)[None, :, None],
            lists[None],
            0,
        ),
        axis=1,
    )
    pairs = head_count // 2
    pair_used = jnp.max(is_temporal.reshape(pairs, 2), axis=1)
    order = jnp.cumsum(pair_used) - 1
    last = jnp.max(jnp.where(pair_used == 1, jnp.arange(pairs), 0))
    visits = jnp.sum(
        jnp.where(
            (order[None, :] == jnp.arange(pairs)[:, None]) & (pair_used[None, :] == 1),
            jnp.arange(pairs)[None, :],
            0,
        ),
        axis=1,
    )
    visits = jnp.where(jnp.arange(pairs) < jnp.sum(pair_used), visits, last).astype(jnp.int32)
    tensors = (queries, key_states, value_states)

    def exchange(array):
        return lax.all_to_all(array, "frame", split_axis=0, concat_axis=0, tiled=True)

    def none_temporal(tensors, old_feature, classes, slots, visits, heads, lists):
        made = ()
        for frame in range(frames_dev):
            made = spatial_call(frame, classes, *tensors, old_feature, made)
        return tuple(made)

    def some_temporal(slot_pairs):
        def run(tensors, old_feature, classes, slots, visits, heads, lists):
            arrived, temporal = [], []
            made = ()
            beside = [[] for _ in range(slot_pairs + 1)]
            for frame in range(frames_dev):
                beside[min(frame, slot_pairs - 1)].append(frame)
            waited = ()
            for at in range(slot_pairs):
                packed = pack_call(1, sources, heads[2 * at : 2 * at + 2], tensors)
                packed, waited = lax.optimization_barrier((packed, waited))
                got = exchange(packed)
                if at > 0:
                    own_lists = lists[2 * at - 2 : 2 * at].reshape(-1)
                    temporal = [
                        temporal_call(own_lists, arrived[-1], slot_pairs - 1, at - 1, temporal)
                    ]
                for frame in beside[at]:
                    made = spatial_call(frame, classes, *tensors, old_feature, made)
                waited = (tuple(temporal), tuple(made))
                got, waited = lax.optimization_barrier((got, waited))
                temporal, made = list(waited[0]), waited[1]
                arrived.append(got)
            returned = []
            if temporal:
                several = exchange(temporal[0])
                final = temporal_call(lists[2 * slot_pairs - 2 : 2 * slot_pairs].reshape(-1), arrived[-1])
                several, final = lax.optimization_barrier((several, final))
                returned.append(several)
            else:
                final = temporal_call(lists[:2].reshape(-1), arrived[-1])
            returned.append(exchange(final))
            return tuple(merge_call(classes, slots, visits, *made, old_feature, returned))

        return run

    branches = [none_temporal] + [some_temporal(n + 1) for n in range((head_count + 1) // 2)]
    return lax.switch(
        (count + 1) // 2, branches,
        tensors, old_feature, is_temporal, slots, visits, heads, lists,
    )


def solution(mesh):
    in_specs = (
        P(("groups", "frame"), None, ("head", "pair")),
        P(("groups", "frame"), None, ("head", "pair")),
        P(("groups", "frame"), None, ("head", "pair")),
        P(("groups", "frame"), None, ("head", "pair")),
        P(),
        P(),
    )
    out_specs = (
        P(("groups", "frame"), None, ("head", "pair")),
        P(("groups", "frame"), None, ("head", "pair")),
    )
    return jax.shard_map(
        per_device, mesh=mesh, in_specs=in_specs, out_specs=out_specs, check_vma=False
    )
```
